256 devices in a mesh: bkt: 32 (over y, z_lo, x), grp: 8 (over z_hi, core).
Axes of the slice: x: 4, y: 4, z: 8 (z_hi: 4, z_lo: 2; z = z_hi * 2 + z_lo), core: 2. Of those that a mesh axis runs over, the one named last changes fastest.
Arguments:
- record_tiles: bfloat16 [49152, 128, 128], P(('bkt', 'grp')), may hold values from 0.0019989014 to 0.049804688
- tile_row: int32 [49152], P(('bkt', 'grp')), may hold values from -1 to 63, as said below
- tile_col: int32 [49152], P(('bkt', 'grp')), may hold values from -1 to 255, as said below
- move_blocks: int32 [256, 64], P('bkt', 'grp'), may hold values 0 or 1
- pairing: int32 [256], replicated, may hold values from 0 to 255, as said below
Outputs:
- updated_panel: float32 [256, 32768], P('bkt', 'grp')
- gains: float32 [256, 64, 128], P('bkt', 'grp')
The draws below stay inside these ranges and needn't reach their ends.
Inputs may be any that keep to these rules, and one draw needn't show every extreme that they name: On each device the live slots come first and no pair (tile_row, tile_col) appears twice; a device has 192, 96, 48 or 24 live slots, and some device has all 192; an empty slot has -1 here and in tile_col. `tile_col`: -1 exactly where tile_row is -1. `pairing`: an involution without fixed points. With owner(b) = b // 8, bucket b pairs with a bucket of the same position b % 8 within its owner, and the 8 buckets of one owner pair with buckets of 8 different owners.
All inputs are finite; a program needn't handle non-finite values. No bound on the sum of `move_blocks` on one device may be relied on, other than what follows from the above.
Results may differ from the reference program's by a relative error of at most 0.0003.
Values may be sent and summed in bfloat16 or wider, within the bound.
A program may use at most 64 MiB of HBM per device.

```python
import math
import jax
import jax.numpy as jnp
from jax import lax

BPO = 8
TILE = 128
RTG = 8
QT = 256
KT = 192
B = 256
RT = 64
SLOTS = 49152
N_BKT = 32
N_GRP = 8


def tile_layout(key):
    base = jax.random.fold_in(key, 11)
    key_perm, key_shift, key_full = jax.random.split(base, 3)
    devices_all = SLOTS // KT
    pair_count = BPO * RTG * QT

    def pick_pairs(sub_key):
        return jax.random.permutation(sub_key, pair_count)[:KT]
    picks = jax.vmap(pick_pairs)(jax.random.split(key_perm, devices_all))
    shifts = jax.random.randint(key_shift, (devices_all,), 0, 4)
    live_count = KT // jnp.left_shift(jnp.ones((devices_all,), jnp.int32), shifts)
    full_device = jax.random.randint(key_full, (), 0, devices_all)
    live_count = jnp.where(jnp.arange(devices_all) == full_device, KT, live_count)
    live_mask = jnp.arange(KT)[None, :] < live_count[:, None]
    rows = jnp.where(live_mask, picks // QT, -1)
    cols = jnp.where(live_mask, picks % QT, -1)
    return (rows.reshape(SLOTS).astype(jnp.int32), cols.reshape(SLOTS).astype(jnp.int32))


def draw_tile_row(key, part):
    return tile_layout(key)[0]


def draw_tile_col(key, part):
    return tile_layout(key)[1]


def draw_pairing(key, part):
    base = jax.random.fold_in(key, 23)
    key_offset, key_label = jax.random.split(base)
    owners = B // BPO
    offsets = jax.random.permutation(key_offset, owners - 1)[:BPO] + 1
    labels = jax.random.permutation(key_label, owners)
    inverse = jnp.argsort(labels)
    bucket = jnp.arange(B)
    owner = bucket // BPO
    position = bucket % BPO
    partner_owner = inverse[jnp.bitwise_xor(labels[owner], offsets[position])]
    return (partner_owner * BPO + position).astype(jnp.int32)


def place_ends(array, own_key, low, top_value):
    spot = [jax.random.randint(jax.random.fold_in(own_key, axis), (), 0, length) for axis, length in enumerate(array.shape)]
    widest = array.shape.index(max(array.shape))
    neighbour = spot[:widest] + [(spot[widest] + 1) % array.shape[widest]] + spot[widest + 1:]
    return array.at[tuple(spot)].set(low).at[tuple(neighbour)].set(top_value)


def steps_of(rng, shape, cuts, least, top_value):
    def one(dim, parts):
        steps = jax.random.uniform(jax.random.fold_in(jax.random.fold_in(rng, 6), dim), (parts,), jnp.float32, least / len(cuts), top_value / len(cuts))
        return jnp.repeat(jnp.exp(steps), shape[dim] // parts).reshape((-1,) + (1,) * (len(shape) - dim - 1))

    loudness = one(*cuts[0])
    for cut in cuts[1:]:
        loudness = loudness * one(*cut)
    return loudness


def setup_inputs(seed: int = 0) -> dict:
    splits = jax.random.split(jax.random.key(seed), 6)
    record_tiles = jnp.clip(jnp.exp(math.log(0.049804688) - 3.2155114 * jax.random.uniform(splits[0], (SLOTS, TILE, TILE), jnp.float32) ** steps_of(splits[0], (SLOTS, TILE, TILE), ((0, 256),), -0.2, 0.2)), 0.0019989014, 0.049804688).astype(jnp.bfloat16)
    tile_row = draw_tile_row(jax.random.fold_in(splits[5], 71), 0)
    tile_col = draw_tile_col(jax.random.fold_in(splits[5], 71), 0)
    move_blocks = place_ends((jax.random.randint(splits[3], (B, RT), 0, 3) < 1).astype(jnp.int32), jax.random.fold_in(splits[3], 1), 0, 1)
    pairing = draw_pairing(jax.random.fold_in(splits[5], 71), 0)
    return {"record_tiles": record_tiles, "tile_row": tile_row, "tile_col": tile_col, "move_blocks": move_blocks, "pairing": pairing}


survival_rate = 0.5


def locate(device, rows):
    owner = device // N_GRP
    member = device % N_GRP
    live_mask = rows >= 0
    row_index = jnp.where(live_mask, rows, 0).astype(jnp.int32)
    bucket = (owner * BPO + row_index // RTG).astype(jnp.int32)
    block = (member * RTG + row_index % RTG).astype(jnp.int32)
    return live_mask, row_index, bucket, block


def reference(record_tiles, tile_row, tile_col, move_blocks, pairing):
    devices_all = N_BKT * N_GRP
    tiles_dev = record_tiles.reshape(devices_all, KT, TILE, TILE)
    rows_dev = tile_row.reshape(devices_all, KT)
    cols_dev = tile_col.reshape(devices_all, KT)
    index_dev = jnp.arange(devices_all, dtype=jnp.int32)

    def add_counts(carry, items):
        counts, deltas = carry
        tiles, rows, cols, device = items
        live_mask, row_index, bucket, block = locate(device, rows)
        col_index = jnp.where(live_mask, cols, 0).astype(jnp.int32)
        live_float = live_mask.astype(jnp.float32)[:, None]
        column_sums = jnp.sum(tiles.astype(jnp.float32), axis=1) * live_float
        moving = move_blocks[bucket, block].astype(jnp.float32)[:, None]
        counts = counts.at[bucket, col_index].add(column_sums)
        deltas = deltas.at[bucket, col_index].add(column_sums * moving)
        return (counts, deltas), None

    start = (jnp.zeros((B, QT, TILE), jnp.float32), jnp.zeros((B, QT, TILE), jnp.float32))
    (counts, deltas), _ = lax.scan(add_counts, start, (tiles_dev, rows_dev, cols_dev, index_dev))
    panel16 = jnp.exp(-survival_rate * counts).astype(jnp.bfloat16)
    partner16 = panel16[pairing]
    partner_deltas = deltas[pairing]
    updated_panel = jnp.exp(-survival_rate * (counts - deltas + partner_deltas)).reshape(B, QT * TILE)

    def add_gains(carry, items):
        tiles, rows, cols, device = items
        live_mask, row_index, bucket, block = locate(device, rows)
        col_index = jnp.where(live_mask, cols, 0).astype(jnp.int32)
        tiles_wide = tiles.astype(jnp.float32)
        own_rows = panel16[bucket, col_index].astype(jnp.float32)
        other_rows = partner16[bucket, col_index].astype(jnp.float32)
        own_terms = jnp.einsum("krq,kq->kr", tiles_wide, own_rows, precision=lax.Precision.HIGHEST)
        other_terms = jnp.einsum("krq,kq->kr", tiles_wide, other_rows, precision=lax.Precision.HIGHEST)
        weight = live_mask.astype(jnp.float32)[:, None]
        own_sum = jnp.zeros((BPO * RTG, TILE), jnp.float32).at[row_index].add(own_terms * weight)
        other_sum = jnp.zeros((BPO * RTG, TILE), jnp.float32).at[row_index].add(other_terms * weight)
        return carry, survival_rate * (own_sum - other_sum)

    _, per_device = lax.scan(add_gains, jnp.zeros((), jnp.float32), (tiles_dev, rows_dev, cols_dev, index_dev))
    gains = per_device.reshape(N_BKT, N_GRP, BPO, RTG, TILE).transpose(0, 2, 1, 3, 4).reshape(B, RT, TILE)
    return updated_panel, gains
```

```python
import jax
import jax.numpy as jnp
from jax import lax
from jax.experimental import pallas as pl
from jax.experimental.pallas import tpu as pltpu
from jax.sharding import PartitionSpec as P

BPO = 8
TILE = 128
RTG = 8
QT = 256
KT = 192
N_BKT = 32
N_GRP = 8
N_ZH = N_GRP // 2
QM = QT // N_GRP
SEG = BPO * QM
META = 16
BLK = KT + META
CHUNK = 16
N_CHUNK = KT // CHUNK
SUM_SCALE = 10240.0
UNIT_SCALE = 65535.0
HALF = 32768
MOVED = BPO * QT

survival_rate = 0.5
f32 = jnp.float32
bf16 = jnp.bfloat16
i32 = jnp.int32
i16 = jnp.int16


def to_code(values, scale):
    return ((values * scale + 0.5).astype(i32) - HALF).astype(i16)


def iota(shape, dim):
    return lax.broadcasted_iota(i32, shape, dim)


def kernel(
    tiles_hbm, row_ref, col_ref, move_ref, pair_ref,
    panel_ref, gains_ref,
    tiles, wide, gath, acc, own, rows, outbox, inbox, rest, pg, look, terms,
    load_sem, s1, f1, r1, q1, s2, r2, s3, f3, r3, q3,
):
    o = lax.axis_index("bkt")
    h = lax.axis_index("grp")
    zh = h // 2
    core = h % 2
    sibling = zh * 2 + (1 - core)

    def load(c):
        part = pl.ds(c * CHUNK, CHUNK)
        return pltpu.make_async_copy(tiles_hbm.at[part], tiles.at[part], load_sem.at[c])

    @pl.loop(0, N_CHUNK)
    def _(c):
        load(c).start()

    barrier = pltpu.get_barrier_semaphore()

    @pl.loop(1, N_BKT)
    def _(d):
        pl.semaphore_signal(barrier, inc=1, device_id=((o + d) % N_BKT, h), device_id_type=pl.DeviceIdType.MESH)

    @pl.loop(1, N_ZH)
    def _(d):
        peer = ((zh + d) % N_ZH) * 2 + core
        pl.semaphore_signal(barrier, inc=1, device_id=(o, peer), device_id_type=pl.DeviceIdType.MESH)

    pl.semaphore_signal(barrier, inc=1, device_id=(o, sibling), device_id_type=pl.DeviceIdType.MESH)

    row = row_ref[...]
    live = row >= 0
    seg_row = jnp.where(live, (row >> 3) * QT + col_ref[...], -1)
    moving = jnp.zeros_like(row)
    for r in range(BPO * RTG):
        moving = jnp.where(row == r, move_ref[r // RTG, r % RTG], moving)
    wide[...] = jnp.full(wide.shape, -1, i32)
    wide[:, :KT] = jnp.where(live, seg_row + MOVED * moving, -1)
    place = iota((META, TILE), 0)
    meta = jnp.where(place == 0, wide[:, :TILE], jnp.where(place == 1, wide[:, TILE:], -1))
    gath[h, KT:BLK, :] = meta.astype(i16)
    diagonal = iota((KT, KT), 0) == iota((KT, KT), 1)
    seg_col = jnp.sum(jnp.where(diagonal, seg_row.astype(f32), 0.0), axis=1, keepdims=True).astype(i32)

    @pl.loop(0, N_CHUNK)
    def _(c):
        load(c).wait()
        sums = jnp.sum(tiles[pl.ds(c * CHUNK, CHUNK)].astype(f32), axis=1)
        gath[h, pl.ds(c * CHUNK, CHUNK), :] = to_code(sums, SUM_SCALE)

    pl.semaphore_wait(barrier, (N_BKT - 1) + (N_ZH - 1) + 1)

    def direct(buf, j, send, recv):
        peer = ((zh + j) % N_ZH) * 2 + core
        return pltpu.make_async_remote_copy(
            src_ref=buf.at[h], dst_ref=buf.at[h], send_sem=send.at[j], recv_sem=recv.at[j],
            device_id=(o, peer), device_id_type=pl.DeviceIdType.MESH,
        )

    def arrived(j):
        return ((zh + N_ZH - j) % N_ZH) * 2 + core

    def arrived_other(j):
        return ((zh + N_ZH - j) % N_ZH) * 2 + (1 - core)

    def pass_on(buf, j, send, recv):
        return pltpu.make_async_remote_copy(
            src_ref=buf.at[arrived(j)], dst_ref=buf.at[arrived(j)], send_sem=send.at[j], recv_sem=recv.at[j],
            device_id=(o, sibling), device_id_type=pl.DeviceIdType.MESH,
        )

    def gather(buf, send, forward, recv, other, use):
        for j in range(1, N_ZH):
            direct(buf, j, send, recv).start()

        @pl.loop(0, N_ZH)
        def _(j):
            @pl.when(j > 0)
            def _():
                pltpu.make_async_remote_copy(
                    src_ref=buf.at[arrived(j)], dst_ref=buf.at[arrived(j)], send_sem=send.at[j], recv_sem=recv.at[j],
                    device_id=(o, sibling), device_id_type=pl.DeviceIdType.MESH,
                ).wait_recv()

            pass_on(buf, j, forward, other).start()
            use(arrived(j))

        @pl.loop(0, N_ZH)
        def _(j):
            pltpu.make_async_remote_copy(
                src_ref=buf.at[arrived_other(j)], dst_ref=buf.at[arrived_other(j)], send_sem=forward.at[j],
                recv_sem=other.at[j], device_id=(o, sibling), device_id_type=pl.DeviceIdType.MESH,
            ).wait_recv()
            use(arrived_other(j))

    def gather_sent(buf, send, forward, recv, other):
        for j in range(1, N_ZH):
            direct(buf, j, send, recv).wait_send()
        for j in range(N_ZH):
            pass_on(buf, j, forward, other).wait_send()

    acc[...] = jnp.zeros_like(acc)
    place = iota((SEG, KT), 0)
    wanted = (place // QM) * QT + h * QM + place % QM

    def count(m):
        code = gath[m, 0:KT, :].astype(i32) + HALF
        high = (code >> 8).astype(f32).astype(bf16)
        low = (code & 255).astype(f32).astype(bf16)
        parts = jnp.concatenate([high, low], axis=1)
        meta = gath[m, KT:BLK, :].astype(i32)
        theirs = jnp.concatenate([meta[0:1], meta[1:2]], axis=1)[:, :KT]
        moved = theirs >= MOVED
        seg = jnp.where(moved, theirs - MOVED, theirs)
        hit = jnp.where(wanted == seg, 1.0, 0.0)
        hit_moved = jnp.where(moved, hit, 0.0)
        mine = jnp.where(seg_col == seg, 1.0, 0.0)
        table = jnp.concatenate([hit, hit_moved, mine], axis=0).astype(bf16)
        acc[...] += jnp.dot(table, parts, preferred_element_type=f32)

    gather(gath, s1, f1, r1, q1, count)

    total = acc[:, :TILE] * (256.0 / SUM_SCALE) + acc[:, TILE:] * (1.0 / SUM_SCALE)
    counts = total[:SEG]
    deltas = total[SEG : 2 * SEG]
    panel_code = to_code(jnp.exp(-survival_rate * counts), UNIT_SCALE).reshape(BPO, QM, TILE)
    delta_code = to_code(jnp.exp(-survival_rate * deltas), UNIT_SCALE).reshape(BPO, QM, TILE)
    rows[:, 0:QM, :] = panel_code
    rows[:, QM : 2 * QM, :] = delta_code

    partner_owner = [pair_ref[o * BPO + p] // BPO for p in range(BPO)]

    def swap(d):
        return pltpu.make_async_remote_copy(
            src_ref=outbox.at[d - 1], dst_ref=inbox.at[d - 1], send_sem=s2.at[d - 1], recv_sem=r2.at[d - 1],
            device_id=((o + d) % N_BKT, h), device_id_type=pl.DeviceIdType.MESH,
        )

    @pl.loop(1, N_BKT)
    def _(d):
        to = (o + d) % N_BKT
        pick = 0
        for p in range(BPO):
            pick = jnp.where(partner_owner[p] == to, p, pick)
        outbox[d - 1] = rows[pick]
        swap(d).start()

    rest[...] = jnp.exp(-survival_rate * (counts - deltas))
    own[...] = jnp.exp(-survival_rate * total[2 * SEG :]).astype(bf16).astype(f32)
    look[...] = jnp.zeros_like(look)

    @pl.loop(1, N_BKT)
    def _(d):
        swap(d).wait_recv()

    for p in range(BPO):
        part = slice(p * QM, (p + 1) * QM)
        got = inbox[jnp.maximum((o - partner_owner[p] + N_BKT) % N_BKT - 1, 0)].astype(i32) + HALF
        got = got.astype(f32) * (1.0 / UNIT_SCALE)
        pg[h, part, :] = got[:QM].astype(bf16)
        panel_ref[part, :] = rest[part, :] * got[QM:]

    place3 = iota((KT, SEG), 1)
    base = (place3 // QM) * QT + place3 % QM

    def fetch(m):
        table = jnp.where(base == seg_col - m * QM, 1.0, 0.0).astype(bf16)
        look[...] += jnp.dot(table, pg[m], preferred_element_type=f32)

    gather(pg, s3, f3, r3, q3, fetch)

    lane = iota((2 * RTG, TILE), 0)

    @pl.loop(0, KT // RTG)
    def _(g):
        k = pl.multiple_of(g * RTG, RTG)
        pair = jnp.concatenate([own[pl.ds(k, RTG), :], look[pl.ds(k, RTG), :]], axis=0).astype(bf16)
        both = jnp.zeros((2 * RTG, TILE), f32)
        for i in range(RTG):
            got = lax.dot_general(
                pair, tiles[k + i], (((1,), (1,)), ((), ())), preferred_element_type=f32
            )
            both = jnp.where(lane % RTG == i, got, both)
        terms[pl.ds(k, RTG), :] = both[:RTG] - both[RTG:]

    spread = jnp.where(iota((BPO * RTG, KT), 0) == row, 1.0, 0.0)
    gains_ref[...] = survival_rate * jnp.dot(
        spread, terms[...], precision=lax.Precision.HIGHEST, preferred_element_type=f32
    )

    gather_sent(gath, s1, f1, r1, q1)
    gather_sent(pg, s3, f3, r3, q3)

    @pl.loop(1, N_BKT)
    def _(d):
        swap(d).wait_send()


def local(record_tiles, tile_row, tile_col, move_blocks, pairing):
    vmem = pl.BlockSpec(memory_space=pltpu.VMEM)
    smem = pl.BlockSpec(memory_space=pltpu.SMEM)
    dma = pltpu.SemaphoreType.DMA
    panel, gains = pl.pallas_call(
        kernel,
        out_shape=(
            jax.ShapeDtypeStruct((SEG, TILE), f32),
            jax.ShapeDtypeStruct((BPO * RTG, TILE), f32),
        ),
        in_specs=[pl.BlockSpec(memory_space=pl.ANY), vmem, vmem, smem, smem],
        out_specs=(vmem, vmem),
        scratch_shapes=[
            pltpu.VMEM((KT, TILE, TILE), bf16),
            pltpu.VMEM((1, 2 * TILE), i32),
            pltpu.VMEM((N_GRP, BLK, TILE), i16),
            pltpu.VMEM((2 * SEG + KT, 2 * TILE), f32),
            pltpu.VMEM((KT, TILE), f32),
            pltpu.VMEM((BPO, 2 * QM, TILE), i16),
            pltpu.VMEM((N_BKT - 1, 2 * QM, TILE), i16),
            pltpu.VMEM((N_BKT - 1, 2 * QM, TILE), i16),
            pltpu.VMEM((SEG, TILE), f32),
            pltpu.VMEM((N_GRP, SEG, TILE), bf16),
            pltpu.VMEM((KT, TILE), f32),
            pltpu.VMEM((KT, TILE), f32),
            dma((N_CHUNK,)),
            dma((N_ZH,)), dma((N_ZH,)), dma((N_ZH,)), dma((N_ZH,)),
            dma((N_BKT - 1,)), dma((N_BKT - 1,)),
            dma((N_ZH,)), dma((N_ZH,)), dma((N_ZH,)), dma((N_ZH,)),
        ],
        compiler_params=pltpu.CompilerParams(
            collective_id=0, has_side_effects=True, vmem_limit_bytes=60 * 1024 * 1024
        ),
        name="swap_round",
    )(record_tiles, tile_row.reshape(1, KT), tile_col.reshape(1, KT), move_blocks, pairing)
    return panel.reshape(BPO, QM * TILE), gains.reshape(BPO, RTG, TILE)


def solution(mesh):
    placed = (
        P(("bkt", "grp"), None, None),
        P(("bkt", "grp")),
        P(("bkt", "grp")),
        P("bkt", "grp"),
        P(),
    )
    return jax.shard_map(
        local,
        mesh=mesh,
        in_specs=placed,
        out_specs=(P("bkt", "grp"), P("bkt", "grp", None)),
        check_vma=False,
    )
```

```python
import jax
import jax.numpy as jnp
from jax import lax
from jax.experimental import pallas as pl
from jax.experimental.pallas import tpu as pltpu
from jax.sharding import PartitionSpec as P

BPO = 8
TILE = 128
RTG = 8
QT = 256
KT = 192
N_BKT = 32
N_GRP = 8
N_ZH = N_GRP // 2
QM = QT // N_GRP
SEG = BPO * QM
META = 16
BLK = KT + META
CHUNK = 32
N_CHUNK = KT // CHUNK
SUM_SCALE = 10240.0
UNIT_SCALE = 65535.0
HALF = 32768
MOVED = BPO * QT
VMEM_BYTES = 57 * 1024 * 1024

survival_rate = 0.5
f32 = jnp.float32
bf16 = jnp.bfloat16
i32 = jnp.int32
i16 = jnp.int16


def to_code(values, scale):
    return ((values * scale + 0.5).astype(i32) - HALF).astype(i16)


def iota(shape, dim):
    return lax.broadcasted_iota(i32, shape, dim)


def kernel(
    tiles_hbm, row_hbm, col_hbm, move_hbm, pair_hbm,
    panel_ref, gains_ref,
    row_ref, col_ref, move_ref, pair_ref, pick_ref,
    tiles, turned, wide, gath, acc, own, panels, factors, panel_out, far_out, factor_out, panel_in, far_in, factor_in,
    rest, pg, look, terms,
    load_sem, small_sem, s1, f1, r1, q1, s2, r2, s5, r5, s4, r4, s3, f3, r3, q3,
):
    o = lax.axis_index("bkt")
    h = lax.axis_index("grp")
    zh = h // 2
    core = h % 2
    sibling = zh * 2 + (1 - core)

    def far_first(i):
        return (2 + i) * (1 - i // 2) + (3 - i) * (i // 2)

    def owner_at(d):
        y = (o // 8 + far_first(d // 8)) % 4
        z = (o // 4 + 1 - d % 2) % 2
        x = (o + far_first((d // 2) % 4)) % 4
        return y * 8 + z * 4 + x

    def load(c):
        part = pl.ds(c * CHUNK, CHUNK)
        return pltpu.make_async_copy(tiles_hbm.at[part], tiles.at[part], load_sem.at[c])

    small = [
        pltpu.make_async_copy(src, dst, small_sem.at[i])
        for i, (src, dst) in enumerate(
            ((row_hbm, row_ref), (col_hbm, col_ref), (move_hbm, move_ref), (pair_hbm, pair_ref))
        )
    ]
    for copy in small:
        copy.start()

    @pl.loop(0, N_CHUNK)
    def _(c):
        load(c).start()

    barrier = pltpu.get_barrier_semaphore()

    for j in (2, 1, 3):
        peer = ((zh + j) % N_ZH) * 2 + core
        pl.semaphore_signal(barrier, inc=1, device_id=(o, peer), device_id_type=pl.DeviceIdType.MESH)

    @pl.loop(0, N_BKT - 1)
    def _(d):
        pl.semaphore_signal(barrier, inc=1, device_id=(owner_at(d), h), device_id_type=pl.DeviceIdType.MESH)

    pl.semaphore_signal(barrier, inc=1, device_id=(o, sibling), device_id_type=pl.DeviceIdType.MESH)

    for copy in small:
        copy.wait()

    row = row_ref[...]
    live = row >= 0
    seg_row = jnp.where(live, (row >> 3) * QT + col_ref[...], -1)
    moving = jnp.zeros_like(row)
    for r in range(BPO * RTG):
        moving = jnp.where(row == r, move_ref[r // RTG, r % RTG], moving)
    wide[...] = jnp.full(wide.shape, -1, i32)
    wide[:, :KT] = jnp.where(live, seg_row + MOVED * moving, -1)
    place = iota((META, TILE), 0)
    meta = jnp.where(place == 0, wide[:, :TILE], jnp.where(place == 1, wide[:, TILE:], -1))
    gath[h, 0:META, :] = meta.astype(i16)

    panel_in[o] = jnp.zeros(panel_in.shape[1:], bf16)
    far_in[o] = jnp.zeros(far_in.shape[1:], bf16)
    factor_in[o] = jnp.zeros(factor_in.shape[1:], i16)

    def column_sums(c):
        load(c).wait()

        @pl.loop(0, CHUNK // META)
        def _(e):
            k = pl.multiple_of(c * CHUNK + e * META, META)
            sums = jnp.sum(tiles[pl.ds(k, META)].astype(f32), axis=1)
            gath[h, pl.ds(META + k, META), :] = to_code(sums, SUM_SCALE)

    order = (2, 1, 3)

    def arrived(j):
        return ((zh + N_ZH - j) % N_ZH) * 2 + core

    def arrived_other(j):
        return ((zh + N_ZH - j) % N_ZH) * 2 + (1 - core)

    def hop(buf, part, block, to, send_sem, recv_sem):
        ref = buf.at[block, part]
        return pltpu.make_async_remote_copy(
            src_ref=ref, dst_ref=ref, send_sem=send_sem, recv_sem=recv_sem,
            device_id=(o, to), device_id_type=pl.DeviceIdType.MESH,
        )

    def send_own(buf, part, x, send, forward, recv, other):
        for j in order:
            hop(buf, part, h, ((zh + j) % N_ZH) * 2 + core, send.at[x, j], recv.at[x, j]).start()
        hop(buf, part, h, sibling, forward.at[x, 0], other.at[x, 0]).start()

    def pass_on(buf, part, x, j, send, forward, recv, other):
        hop(buf, part, arrived(j), sibling, send.at[x, j], recv.at[x, j]).wait_recv()
        hop(buf, part, arrived(j), sibling, forward.at[x, j], other.at[x, j]).start()

    def from_other(buf, part, x, j, forward, other):
        hop(buf, part, arrived_other(j), sibling, forward.at[x, j], other.at[x, j]).wait_recv()

    def all_sent(buf, part, x, send, forward, recv, other):
        for j in order:
            hop(buf, part, h, ((zh + j) % N_ZH) * 2 + core, send.at[x, j], recv.at[x, j]).wait_send()
        for j in range(N_ZH):
            hop(buf, part, arrived(j), sibling, forward.at[x, j], other.at[x, j]).wait_send()

    def in_order(i):
        return i + (i // 2) * (5 - 2 * i)

    first = (gath, pl.ds(0, BLK), 0, s1, f1, r1, q1)

    for c in range(N_CHUNK):
        column_sums(c)
    pl.semaphore_wait(barrier, (N_BKT - 1) + (N_ZH - 1) + 1)
    send_own(*first)

    diagonal = iota((KT, KT), 0) == iota((KT, KT), 1)
    seg_col = jnp.sum(jnp.where(diagonal, seg_row.astype(f32), 0.0), axis=1, keepdims=True).astype(i32)
    acc[...] = jnp.zeros_like(acc)
    place = iota((SEG, KT), 0)
    far = arrived(2)
    wanted = (place // QM) * QT + h * QM + place % QM
    wanted_far = wanted + (far - h) * QM

    partner_owner = [pair_ref[o * BPO + p] // BPO for p in range(BPO)]

    @pl.loop(0, N_BKT - 1)
    def _(d):
        to = owner_at(d)
        pick = 0
        for p in range(BPO):
            pick = jnp.where(partner_owner[p] == to, p, pick)
        pick_ref[d] = pick

    def count(m):
        code = gath[m, META:BLK, :].astype(i32) + HALF
        high = (code >> 8).astype(f32).astype(bf16)
        low = (code & 255).astype(f32).astype(bf16)
        parts = jnp.concatenate([high, low], axis=1)
        meta = gath[m, 0:META, :].astype(i32)
        theirs = jnp.concatenate([meta[0:1], meta[1:2]], axis=1)[:, :KT]
        moved = theirs >= MOVED
        seg = jnp.where(moved, theirs - MOVED, theirs)
        hit = jnp.where(wanted == seg, 1.0, 0.0)
        hit_moved = jnp.where(moved, hit, 0.0)
        hit_far = jnp.where(wanted_far == seg, 1.0, 0.0)
        mine = jnp.where(seg_col == seg, 1.0, 0.0)
        table = jnp.concatenate([hit, hit_far, hit_moved, mine], axis=0).astype(bf16)
        acc[...] += jnp.dot(table, parts, preferred_element_type=f32)

    @pl.loop(0, KT // 4)
    def _(g):
        for b in range(2):
            for a in range(2):
                turned[g, a * TILE : (a + 1) * TILE, b * TILE : (b + 1) * TILE] = tiles[4 * g + 2 * b + a].T

    @pl.loop(0, N_ZH)
    def _(i):
        count(arrived(in_order(i)))

        @pl.when(i < N_ZH - 1)
        def _():
            j = in_order(i + 1)
            pass_on(*first[:3], j, *first[3:])

        j = in_order(i)
        from_other(*first[:3], j, f1, q1)
        count(arrived_other(j))

    total = acc[:, :TILE] * (256.0 / SUM_SCALE) + acc[:, TILE:] * (1.0 / SUM_SCALE)
    counts = total[:SEG]
    deltas = total[2 * SEG : 3 * SEG]
    both = jnp.exp(-survival_rate * total[: 2 * SEG]).astype(bf16)
    panels[:, 0:QM, :] = both[:SEG].reshape(BPO, QM, TILE)
    panels[:, QM : 2 * QM, :] = both[SEG:].reshape(BPO, QM, TILE)

    def swap(outbox, inbox, d, send, recv):
        return pltpu.make_async_remote_copy(
            src_ref=outbox.at[d], dst_ref=inbox.at[o], send_sem=send.at[d], recv_sem=recv.at[d],
            device_id=(owner_at(d), h), device_id_type=pl.DeviceIdType.MESH,
        )

    def swapped(inbox, d, send, recv):
        y = (o // 8 + 4 - far_first(d // 8)) % 4
        z = (o // 4 + 1 - d % 2) % 2
        x = (o + 4 - far_first((d // 2) % 4)) % 4
        slot = inbox.at[y * 8 + z * 4 + x]
        return pltpu.make_async_remote_copy(
            src_ref=slot, dst_ref=slot, send_sem=send.at[d], recv_sem=recv.at[d],
            device_id=(owner_at(d), h), device_id_type=pl.DeviceIdType.MESH,
        )

    @pl.loop(0, N_BKT - 1)
    def _(d):
        panel_out[d] = panels[pick_ref[d], 0:QM]
        swap(panel_out, panel_in, d, s2, r2).start()

    @pl.loop(0, N_BKT - 1)
    def _(d):
        far_out[d] = panels[pick_ref[d], QM : 2 * QM]
        swap(far_out, far_in, d, s5, r5).start()

    factors[...] = to_code(jnp.exp(-survival_rate * deltas), UNIT_SCALE).reshape(BPO, QM, TILE)

    rest[...] = jnp.exp(-survival_rate * (counts - deltas))
    own[...] = jnp.exp(-survival_rate * total[3 * SEG :]).astype(bf16).astype(f32)
    look[...] = jnp.zeros_like(look)

    @pl.loop(0, N_BKT - 1)
    def _(d):
        swapped(panel_in, d, s2, r2).wait_recv()

    for p in range(BPO):
        part = slice(p * QM, (p + 1) * QM)
        pg[h, part, :] = panel_in[partner_owner[p]]

    near = (1, 3)
    for j in near:
        hop(pg, pl.ds(0, SEG), h, ((zh + j) % N_ZH) * 2 + core, s3.at[j], r3.at[j]).start()

    def to_other(j):
        return hop(pg, pl.ds(0, SEG), arrived(j), sibling, f3.at[j], q3.at[j])

    def at_other(j):
        return hop(pg, pl.ds(0, SEG), arrived_other(j), sibling, f3.at[j], q3.at[j])

    to_other(0).start()

    @pl.loop(0, N_BKT - 1)
    def _(d):
        swapped(far_in, d, s5, r5).wait_recv()

    for p in range(BPO):
        pg[far, p * QM : (p + 1) * QM, :] = far_in[partner_owner[p]]

    to_other(2).start()

    @pl.loop(0, N_BKT - 1)
    def _(d):
        factor_out[d] = factors[pick_ref[d]]
        swap(factor_out, factor_in, d, s4, r4).start()

    place3 = iota((KT, SEG), 1)
    base = (place3 // QM) * QT + place3 % QM

    def fetch(m):
        table = jnp.where(base == seg_col - m * QM, 1.0, 0.0).astype(bf16)
        look[...] += jnp.dot(table, pg[m], preferred_element_type=f32)

    @pl.loop(0, 2)
    def _(i):
        fetch(arrived(2 * i))
        at_other(2 * i).wait_recv()
        fetch(arrived_other(2 * i))

    for j in near:
        hop(pg, pl.ds(0, SEG), arrived(j), sibling, s3.at[j], r3.at[j]).wait_recv()
        to_other(j).start()

    @pl.loop(0, 2)
    def _(i):
        fetch(arrived(2 * i + 1))

    @pl.loop(0, 2)
    def _(i):
        at_other(2 * i + 1).wait_recv()
        fetch(arrived_other(2 * i + 1))

    lane = iota((2 * RTG, TILE), 0) % RTG
    even = lane % 2 == 0
    across = (lane // 2) % 2
    down = lane // 4

    @pl.loop(0, KT // (4 * RTG))
    def _(g):
        for x in range(4):
            k = pl.multiple_of(g * 4 * RTG + x * RTG, RTG)
            pair = jnp.concatenate([own[pl.ds(k, RTG), :], look[pl.ds(k, RTG), :]], axis=0)
            split = jnp.concatenate([jnp.where(even, pair, 0.0), jnp.where(even, 0.0, pair)], axis=1).astype(bf16)
            both = jnp.zeros((2 * RTG, TILE), f32)
            for y in range(2):
                got = jnp.dot(split, turned[g * RTG + x * 2 + y], preferred_element_type=f32)
                got = jnp.where(across == 0, got[:, :TILE], got[:, TILE:])
                both = jnp.where(down == y, got, both)
            terms[pl.ds(k, RTG), :] = both[:RTG] - both[RTG:]

    spread = jnp.where(iota((BPO * RTG, KT), 0) == row, 1.0, 0.0).astype(bf16)
    term = terms[...]
    high = term.astype(bf16)
    term = term - high.astype(f32)
    mid = term.astype(bf16)
    low = (term - mid.astype(f32)).astype(bf16)
    summed = jnp.dot(spread, jnp.concatenate([high, mid, low], axis=1), preferred_element_type=f32)
    gains_ref[...] = survival_rate * (summed[:, :TILE] + summed[:, TILE : 2 * TILE] + summed[:, 2 * TILE :])

    @pl.loop(0, N_BKT - 1)
    def _(d):
        swapped(factor_in, d, s4, r4).wait_recv()

    for p in range(BPO):
        part = slice(p * QM, (p + 1) * QM)
        got = (factor_in[partner_owner[p]].astype(i32) + HALF).astype(f32) * (1.0 / UNIT_SCALE)
        rest[part, :] = rest[part, :] * got

    for t in range(QM):
        panel_ref[:, t * TILE : (t + 1) * TILE] = rest[pl.ds(t, BPO, stride=QM), :]

    all_sent(*first)
    for j in near:
        hop(pg, pl.ds(0, SEG), h, ((zh + j) % N_ZH) * 2 + core, s3.at[j], r3.at[j]).wait_send()
    for j in range(N_ZH):
        to_other(j).wait_send()

    @pl.loop(0, N_BKT - 1)
    def _(d):
        swap(panel_out, panel_in, d, s2, r2).wait_send()
        swap(far_out, far_in, d, s5, r5).wait_send()
        swap(factor_out, factor_in, d, s4, r4).wait_send()


def hand_over(panel_ref, gains_ref, panel_out, gains_out):
    panel_out[...] = panel_ref[...]
    gains_out[...] = gains_ref[...]


def local(record_tiles, tile_row, tile_col, move_blocks, pairing):
    vmem = pl.BlockSpec(memory_space=pltpu.VMEM)
    hbm = pl.BlockSpec(memory_space=pltpu.HBM)
    dma = pltpu.SemaphoreType.DMA
    panel, gains = pl.pallas_call(
        kernel,
        out_shape=(
            jax.ShapeDtypeStruct((BPO, QM * TILE), f32),
            jax.ShapeDtypeStruct((BPO * RTG, TILE), f32),
        ),
        in_specs=[hbm] * 5,
        out_specs=(vmem, vmem),
        scratch_shapes=[
            pltpu.VMEM((1, KT), i32),
            pltpu.VMEM((1, KT), i32),
            pltpu.SMEM((BPO, RTG), i32),
            pltpu.SMEM((N_BKT * BPO,), i32),
            pltpu.SMEM((N_BKT,), i32),
            pltpu.VMEM((KT, TILE, TILE), bf16),
            pltpu.VMEM((KT // 4, 2 * TILE, 2 * TILE), bf16),
            pltpu.VMEM((1, 2 * TILE), i32),
            pltpu.VMEM((N_GRP, BLK, TILE), i16),
            pltpu.VMEM((3 * SEG + KT, 2 * TILE), f32),
            pltpu.VMEM((KT, TILE), f32),
            pltpu.VMEM((BPO, 2 * QM, TILE), bf16),
            pltpu.VMEM((BPO, QM, TILE), i16),
            pltpu.VMEM((N_BKT - 1, QM, TILE), bf16),
            pltpu.VMEM((N_BKT - 1, QM, TILE), bf16),
            pltpu.VMEM((N_BKT - 1, QM, TILE), i16),
            pltpu.VMEM((N_BKT, QM, TILE), bf16),
            pltpu.VMEM((N_BKT, QM, TILE), bf16),
            pltpu.VMEM((N_BKT, QM, TILE), i16),
            pltpu.VMEM((SEG, TILE), f32),
            pltpu.VMEM((N_GRP, SEG, TILE), bf16),
            pltpu.VMEM((KT, TILE), f32),
            pltpu.VMEM((KT, TILE), f32),
            dma((N_CHUNK,)),
            dma((4,)),
            dma((1, N_ZH)), dma((1, N_ZH)), dma((1, N_ZH)), dma((1, N_ZH)),
            dma((N_BKT - 1,)), dma((N_BKT - 1,)), dma((N_BKT - 1,)),
            dma((N_BKT - 1,)), dma((N_BKT - 1,)), dma((N_BKT - 1,)),
            dma((N_ZH,)), dma((N_ZH,)), dma((N_ZH,)), dma((N_ZH,)),
        ],
        compiler_params=pltpu.CompilerParams(
            collective_id=0, has_side_effects=True, vmem_limit_bytes=VMEM_BYTES
        ),
        name="swap_round",
    )(record_tiles, tile_row.reshape(1, KT), tile_col.reshape(1, KT), move_blocks, pairing)
    return pl.pallas_call(
        hand_over,
        out_shape=(
            jax.ShapeDtypeStruct((BPO, QM * TILE), f32),
            jax.ShapeDtypeStruct((BPO, RTG, TILE), f32),
        ),
        in_specs=[vmem, vmem],
        out_specs=(vmem, vmem),
        compiler_params=pltpu.CompilerParams(vmem_limit_bytes=VMEM_BYTES),
        name="hand_over",
    )(panel, gains.reshape(BPO, RTG, TILE))


def solution(mesh):
    placed = (
        P(("bkt", "grp"), None, None),
        P(("bkt", "grp")),
        P(("bkt", "grp")),
        P("bkt", "grp"),
        P(),
    )
    return jax.shard_map(
        local,
        mesh=mesh,
        in_specs=placed,
        out_specs=(P("bkt", "grp"), P("bkt", "grp", None)),
        check_vma=False,
    )
```

```python
import jax
import jax.numpy as jnp
from jax import lax
from jax.experimental import pallas as pl
from jax.experimental.pallas import tpu as pltpu
from jax.sharding import PartitionSpec as P

BPO = 8
TILE = 128
RTG = 8
QT = 256
KT = 192
N_BKT = 32
N_GRP = 8
N_ZH = N_GRP // 2
QM = QT // N_GRP
SEG = BPO * QM
META = 16
BLK = KT + META
CHUNK = 32
N_CHUNK = KT // CHUNK
SUM_SCALE = 10240.0
UNIT_SCALE = 65535.0
HALF = 32768
MOVED = BPO * QT
VMEM_BYTES = 57 * 1024 * 1024

survival_rate = 0.5
f32 = jnp.float32
bf16 = jnp.bfloat16
i32 = jnp.int32
i16 = jnp.int16


def to_code(values, scale):
    return ((values * scale + 0.5).astype(i32) - HALF).astype(i16)


def iota(shape, dim):
    return lax.broadcasted_iota(i32, shape, dim)


def kernel(
    tiles_hbm, row_hbm, col_hbm, move_hbm, pair_hbm,
    panel_ref, gains_ref,
    row_ref, col_ref, move_ref, pair_ref, pick_ref, slot_ref,
    tiles, turned, wide, gath, acc, own, panels, factors, panel_out, far_out, factor_out, panel_in, far_in, factor_in,
    rest, pg, look, terms,
    load_sem, small_sem, s1, f1, r1, q1, s2, r2, s5, r5, s4, r4, s3, f3, r3, q3,
):
    o = lax.axis_index("bkt")
    h = lax.axis_index("grp")
    zh = h // 2
    core = h % 2
    sibling = zh * 2 + (1 - core)

    def far_first(i):
        return (2 + i) * (1 - i // 2) + (3 - i) * (i // 2)

    def owner_at(d):
        y = (o // 8 + far_first(d // 8)) % 4
        z = (o // 4 + 1 - d % 2) % 2
        x = (o + far_first((d // 2) % 4)) % 4
        return y * 8 + z * 4 + x

    def load(c):
        part = pl.ds(c * CHUNK, CHUNK)
        return pltpu.make_async_copy(tiles_hbm.at[part], tiles.at[part], load_sem.at[c])

    small = [
        pltpu.make_async_copy(src, dst, small_sem.at[i])
        for i, (src, dst) in enumerate(
            ((row_hbm, row_ref), (col_hbm, col_ref), (move_hbm, move_ref), (pair_hbm, pair_ref))
        )
    ]
    for copy in small:
        copy.start()

    @pl.loop(0, N_CHUNK)
    def _(c):
        load(c).start()

    barrier = pltpu.get_barrier_semaphore()

    for j in (2, 1, 3):
        peer = ((zh + j) % N_ZH) * 2 + core
        pl.semaphore_signal(barrier, inc=1, device_id=(o, peer), device_id_type=pl.DeviceIdType.MESH)

    @pl.loop(0, N_BKT - 1)
    def _(d):
        pl.semaphore_signal(barrier, inc=1, device_id=(owner_at(d), h), device_id_type=pl.DeviceIdType.MESH)

    pl.semaphore_signal(barrier, inc=1, device_id=(o, sibling), device_id_type=pl.DeviceIdType.MESH)

    for copy in small:
        copy.wait()

    row = row_ref[...]
    live = row >= 0
    seg_row = jnp.where(live, (row >> 3) * QT + col_ref[...], -1)
    moving = jnp.zeros_like(row)
    for r in range(BPO * RTG):
        moving = jnp.where(row == r, move_ref[r // RTG, r % RTG], moving)
    wide[...] = jnp.full(wide.shape, -1, i32)
    wide[:, :KT] = jnp.where(live, seg_row + MOVED * moving, -1)
    place = iota((META, TILE), 0)
    meta = jnp.where(place == 0, wide[:, :TILE], jnp.where(place == 1, wide[:, TILE:], -1))
    gath[h, 0:META, :] = meta.astype(i16)

    def column_sums(c):
        load(c).wait()

        @pl.loop(0, CHUNK // META)
        def _(e):
            k = pl.multiple_of(c * CHUNK + e * META, META)
            sums = jnp.sum(tiles[pl.ds(k, META)].astype(f32), axis=1)
            gath[h, pl.ds(META + k, META), :] = to_code(sums, SUM_SCALE)

    order = (2, 1, 3)

    def arrived(j):
        return ((zh + N_ZH - j) % N_ZH) * 2 + core

    def arrived_other(j):
        return ((zh + N_ZH - j) % N_ZH) * 2 + (1 - core)

    def hop(buf, part, block, to, send_sem, recv_sem):
        ref = buf.at[block, part]
        return pltpu.make_async_remote_copy(
            src_ref=ref, dst_ref=ref, send_sem=send_sem, recv_sem=recv_sem,
            device_id=(o, to), device_id_type=pl.DeviceIdType.MESH,
        )

    def send_own(buf, part, x, send, forward, recv, other):
        for j in order:
            hop(buf, part, h, ((zh + j) % N_ZH) * 2 + core, send.at[x, j], recv.at[x, j]).start()
        hop(buf, part, h, sibling, forward.at[x, 0], other.at[x, 0]).start()

    def pass_on(buf, part, x, j, send, forward, recv, other):
        hop(buf, part, arrived(j), sibling, send.at[x, j], recv.at[x, j]).wait_recv()
        hop(buf, part, arrived(j), sibling, forward.at[x, j], other.at[x, j]).start()

    def from_other(buf, part, x, j, forward, other):
        hop(buf, part, arrived_other(j), sibling, forward.at[x, j], other.at[x, j]).wait_recv()

    def all_sent(buf, part, x, send, forward, recv, other):
        for j in order:
            hop(buf, part, h, ((zh + j) % N_ZH) * 2 + core, send.at[x, j], recv.at[x, j]).wait_send()
        for j in range(N_ZH):
            hop(buf, part, arrived(j), sibling, forward.at[x, j], other.at[x, j]).wait_send()

    def in_order(i):
        return i + (i // 2) * (5 - 2 * i)

    first = (gath, pl.ds(0, BLK), 0, s1, f1, r1, q1)

    for c in range(N_CHUNK):
        column_sums(c)
    pl.semaphore_wait(barrier, (N_BKT - 1) + (N_ZH - 1) + 1)
    send_own(*first)

    diagonal = iota((KT, KT), 0) == iota((KT, KT), 1)
    seg_col = jnp.sum(jnp.where(diagonal, seg_row.astype(f32), 0.0), axis=1, keepdims=True).astype(i32)
    acc[...] = jnp.zeros_like(acc)
    place = iota((SEG, KT), 0)
    far = arrived(2)
    wanted = (place // QM) * QT + h * QM + place % QM
    wanted_far = wanted + (far - h) * QM

    partner_owner = [pair_ref[o * BPO + p] // BPO for p in range(BPO)]

    slot_ref[o] = 0

    @pl.loop(0, N_BKT - 1)
    def _(d):
        to = owner_at(d)
        pick = 0
        for p in range(BPO):
            pick = jnp.where(partner_owner[p] == to, p, pick)
        pick_ref[d] = pick
        y = (o // 8 + 4 - far_first(d // 8)) % 4
        z = (o // 4 + 1 - d % 2) % 2
        x = (o + 4 - far_first((d // 2) % 4)) % 4
        slot_ref[y * 8 + z * 4 + x] = d

    def count(m):
        code = gath[m, META:BLK, :].astype(i32) + HALF
        high = (code >> 8).astype(f32).astype(bf16)
        low = (code & 255).astype(f32).astype(bf16)
        parts = jnp.concatenate([high, low], axis=1)
        meta = gath[m, 0:META, :].astype(i32)
        theirs = jnp.concatenate([meta[0:1], meta[1:2]], axis=1)[:, :KT]
        moved = theirs >= MOVED
        seg = jnp.where(moved, theirs - MOVED, theirs)
        hit = jnp.where(wanted == seg, 1.0, 0.0)
        hit_moved = jnp.where(moved, hit, 0.0)
        hit_far = jnp.where(wanted_far == seg, 1.0, 0.0)
        mine = jnp.where(seg_col == seg, 1.0, 0.0)
        table = jnp.concatenate([hit, hit_far, hit_moved, mine], axis=0).astype(bf16)
        acc[...] += jnp.dot(table, parts, preferred_element_type=f32)

    @pl.loop(0, KT // 4)
    def _(g):
        for b in range(2):
            for a in range(2):
                turned[g, a * TILE : (a + 1) * TILE, b * TILE : (b + 1) * TILE] = tiles[4 * g + 2 * b + a].T

    @pl.loop(0, N_ZH)
    def _(i):
        count(arrived(in_order(i)))

        @pl.when(i < N_ZH - 1)
        def _():
            j = in_order(i + 1)
            pass_on(*first[:3], j, *first[3:])

        j = in_order(i)
        from_other(*first[:3], j, f1, q1)
        count(arrived_other(j))

    total = acc[:, :TILE] * (256.0 / SUM_SCALE) + acc[:, TILE:] * (1.0 / SUM_SCALE)
    counts = total[:SEG]
    deltas = total[2 * SEG : 3 * SEG]
    both = jnp.exp(-survival_rate * total[: 2 * SEG]).astype(bf16)
    panels[:, 0:QM, :] = both[:SEG].reshape(BPO, QM, TILE)
    panels[:, QM : 2 * QM, :] = both[SEG:].reshape(BPO, QM, TILE)

    def swap(outbox, inbox, d, send, recv):
        return pltpu.make_async_remote_copy(
            src_ref=outbox.at[d], dst_ref=inbox.at[d], send_sem=send.at[0], recv_sem=recv.at[0],
            device_id=(owner_at(d), h), device_id_type=pl.DeviceIdType.MESH,
        )

    def all_swaps(outbox, inbox, send, recv):
        return pltpu.make_async_remote_copy(
            src_ref=outbox, dst_ref=inbox, send_sem=send.at[0], recv_sem=recv.at[0],
            device_id=(owner_at(0), h), device_id_type=pl.DeviceIdType.MESH,
        )

    for d in range(N_BKT - 1):
        panel_out[d] = panels[pick_ref[d], 0:QM]
        swap(panel_out, panel_in, d, s2, r2).start()

    @pl.loop(0, N_BKT - 1)
    def _(d):
        far_out[d] = panels[pick_ref[d], QM : 2 * QM]
        swap(far_out, far_in, d, s5, r5).start()

    factors[...] = to_code(jnp.exp(-survival_rate * deltas), UNIT_SCALE).reshape(BPO, QM, TILE)

    rest[...] = jnp.exp(-survival_rate * (counts - deltas))
    own[...] = jnp.exp(-survival_rate * total[3 * SEG :]).astype(bf16).astype(f32)
    look[...] = jnp.zeros_like(look)

    source = [slot_ref[partner_owner[p]] for p in range(BPO)]
    all_swaps(panel_out, panel_in, s2, r2).wait_recv()

    for p in range(BPO):
        part = slice(p * QM, (p + 1) * QM)
        pg[h, part, :] = panel_in[source[p]]

    near = (1, 3)
    for j in near:
        hop(pg, pl.ds(0, SEG), h, ((zh + j) % N_ZH) * 2 + core, s3.at[j], r3.at[j]).start()

    def to_other(j):
        return hop(pg, pl.ds(0, SEG), arrived(j), sibling, f3.at[j], q3.at[j])

    def at_other(j):
        return hop(pg, pl.ds(0, SEG), arrived_other(j), sibling, f3.at[j], q3.at[j])

    to_other(0).start()

    all_swaps(far_out, far_in, s5, r5).wait_recv()

    for p in range(BPO):
        pg[far, p * QM : (p + 1) * QM, :] = far_in[source[p]]

    to_other(2).start()

    @pl.loop(0, N_BKT - 1)
    def _(d):
        factor_out[d] = factors[pick_ref[d]]
        swap(factor_out, factor_in, d, s4, r4).start()

    place3 = iota((KT, SEG), 1)
    base = (place3 // QM) * QT + place3 % QM

    def fetch(m):
        table = jnp.where(base == seg_col - m * QM, 1.0, 0.0).astype(bf16)
        look[...] += jnp.dot(table, pg[m], preferred_element_type=f32)

    @pl.loop(0, 2)
    def _(i):
        fetch(arrived(2 * i))
        at_other(2 * i).wait_recv()
        fetch(arrived_other(2 * i))

    all_sent(*first)
    all_swaps(panel_out, panel_in, s2, r2).wait_send()
    all_swaps(far_out, far_in, s5, r5).wait_send()
    for j in near:
        hop(pg, pl.ds(0, SEG), arrived(j), sibling, s3.at[j], r3.at[j]).wait_recv()
        to_other(j).start()

    @pl.loop(0, 2)
    def _(i):
        fetch(arrived(2 * i + 1))

    @pl.loop(0, 2)
    def _(i):
        at_other(2 * i + 1).wait_recv()
        fetch(arrived_other(2 * i + 1))

    lane = iota((2 * RTG, TILE), 0) % RTG
    even = lane % 2 == 0
    across = (lane // 2) % 2
    down = lane // 4

    @pl.loop(0, KT // (4 * RTG))
    def _(g):
        for x in range(4):
            k = pl.multiple_of(g * 4 * RTG + x * RTG, RTG)
            pair = jnp.concatenate([own[pl.ds(k, RTG), :], look[pl.ds(k, RTG), :]], axis=0)
            split = jnp.concatenate([jnp.where(even, pair, 0.0), jnp.where(even, 0.0, pair)], axis=1).astype(bf16)
            both = jnp.zeros((2 * RTG, TILE), f32)
            for y in range(2):
                got = jnp.dot(split, turned[g * RTG + x * 2 + y], preferred_element_type=f32)
                got = jnp.where(across == 0, got[:, :TILE], got[:, TILE:])
                both = jnp.where(down == y, got, both)
            terms[pl.ds(k, RTG), :] = both[:RTG] - both[RTG:]

    spread = jnp.where(iota((BPO * RTG, KT), 0) == row, 1.0, 0.0).astype(bf16)
    term = terms[...]
    high = term.astype(bf16)
    term = term - high.astype(f32)
    mid = term.astype(bf16)
    low = (term - mid.astype(f32)).astype(bf16)
    summed = jnp.dot(spread, jnp.concatenate([high, mid, low], axis=1), preferred_element_type=f32)
    gains_ref[...] = survival_rate * (summed[:, :TILE] + summed[:, TILE : 2 * TILE] + summed[:, 2 * TILE :])

    all_swaps(factor_out, factor_in, s4, r4).wait_recv()

    for p in range(BPO):
        part = slice(p * QM, (p + 1) * QM)
        got = (factor_in[source[p]].astype(i32) + HALF).astype(f32) * (1.0 / UNIT_SCALE)
        rest[part, :] = rest[part, :] * got

    for t in range(QM):
        panel_ref[:, t * TILE : (t + 1) * TILE] = rest[pl.ds(t, BPO, stride=QM), :]

    for j in near:
        hop(pg, pl.ds(0, SEG), h, ((zh + j) % N_ZH) * 2 + core, s3.at[j], r3.at[j]).wait_send()
    for j in range(N_ZH):
        to_other(j).wait_send()

    all_swaps(factor_out, factor_in, s4, r4).wait_send()


def hand_over(panel_ref, gains_ref, panel_out, gains_out):
    panel_out[...] = panel_ref[...]
    gains_out[...] = gains_ref[...]


def local(record_tiles, tile_row, tile_col, move_blocks, pairing):
    vmem = pl.BlockSpec(memory_space=pltpu.VMEM)
    hbm = pl.BlockSpec(memory_space=pltpu.HBM)
    dma = pltpu.SemaphoreType.DMA
    panel, gains = pl.pallas_call(
        kernel,
        out_shape=(
            jax.ShapeDtypeStruct((BPO, QM * TILE), f32),
            jax.ShapeDtypeStruct((BPO * RTG, TILE), f32),
        ),
        in_specs=[hbm] * 5,
        out_specs=(vmem, vmem),
        scratch_shapes=[
            pltpu.VMEM((1, KT), i32),
            pltpu.VMEM((1, KT), i32),
            pltpu.SMEM((BPO, RTG), i32),
            pltpu.SMEM((N_BKT * BPO,), i32),
            pltpu.SMEM((N_BKT,), i32),
            pltpu.SMEM((N_BKT,), i32),
            pltpu.VMEM((KT, TILE, TILE), bf16),
            pltpu.VMEM((KT // 4, 2 * TILE, 2 * TILE), bf16),
            pltpu.VMEM((1, 2 * TILE), i32),
            pltpu.VMEM((N_GRP, BLK, TILE), i16),
            pltpu.VMEM((3 * SEG + KT, 2 * TILE), f32),
            pltpu.VMEM((KT, TILE), f32),
            pltpu.VMEM((BPO, 2 * QM, TILE), bf16),
            pltpu.VMEM((BPO, QM, TILE), i16),
            pltpu.VMEM((N_BKT - 1, QM, TILE), bf16),
            pltpu.VMEM((N_BKT - 1, QM, TILE), bf16),
            pltpu.VMEM((N_BKT - 1, QM, TILE), i16),
            pltpu.VMEM((N_BKT - 1, QM, TILE), bf16),
            pltpu.VMEM((N_BKT - 1, QM, TILE), bf16),
            pltpu.VMEM((N_BKT - 1, QM, TILE), i16),
            pltpu.VMEM((SEG, TILE), f32),
            pltpu.VMEM((N_GRP, SEG, TILE), bf16),
            pltpu.VMEM((KT, TILE), f32),
            pltpu.VMEM((KT, TILE), f32),
            dma((N_CHUNK,)),
            dma((4,)),
            dma((1, N_ZH)), dma((1, N_ZH)), dma((1, N_ZH)), dma((1, N_ZH)),
            dma((1,)), dma((1,)), dma((1,)), dma((1,)), dma((1,)), dma((1,)),
            dma((N_ZH,)), dma((N_ZH,)), dma((N_ZH,)), dma((N_ZH,)),
        ],
        compiler_params=pltpu.CompilerParams(
            collective_id=0, has_side_effects=True, vmem_limit_bytes=VMEM_BYTES
        ),
        name="swap_round",
    )(record_tiles, tile_row.reshape(1, KT), tile_col.reshape(1, KT), move_blocks, pairing)
    return pl.pallas_call(
        hand_over,
        out_shape=(
            jax.ShapeDtypeStruct((BPO, QM * TILE), f32),
            jax.ShapeDtypeStruct((BPO, RTG, TILE), f32),
        ),
        in_specs=[vmem, vmem],
        out_specs=(vmem, vmem),
        compiler_params=pltpu.CompilerParams(vmem_limit_bytes=VMEM_BYTES),
        name="hand_over",
    )(panel, gains.reshape(BPO, RTG, TILE))


def solution(mesh):
    placed = (
        P(("bkt", "grp"), None, None),
        P(("bkt", "grp")),
        P(("bkt", "grp")),
        P("bkt", "grp"),
        P(),
    )
    return jax.shard_map(
        local,
        mesh=mesh,
        in_specs=placed,
        out_specs=(P("bkt", "grp"), P("bkt", "grp", None)),
        check_vma=False,
    )
```

```python
import jax
import jax.numpy as jnp
from jax import lax
from jax.experimental import pallas as pl
from jax.experimental.pallas import tpu as pltpu
from jax.sharding import PartitionSpec as P

BPO = 8
TILE = 128
RTG = 8
QT = 256
KT = 192
N_BKT = 32
N_GRP = 8
N_ZH = N_GRP // 2
QM = QT // N_GRP
SEG = BPO * QM
META = 16
BLK = KT + META
CHUNK = 32
N_CHUNK = KT // CHUNK
SUM_SCALE = 10240.0
UNIT_SCALE = 65535.0
HALF = 32768
MOVED = BPO * QT
VMEM_BYTES = 57 * 1024 * 1024

survival_rate = 0.5
f32 = jnp.float32
bf16 = jnp.bfloat16
i32 = jnp.int32
i16 = jnp.int16


def to_code(values, scale):
    return ((values * scale + 0.5).astype(i32) - HALF).astype(i16)


def iota(shape, dim):
    return lax.broadcasted_iota(i32, shape, dim)


def kernel(
    tiles_hbm, row_hbm, col_hbm, move_hbm, pair_hbm,
    panel_ref, gains_ref,
    row_ref, col_ref, move_ref, pair_ref, pick_ref, slot_ref,
    tiles, turned, wide, gath, acc, own, panels, factors, panel_out, far_out, factor_out, panel_in, far_in, factor_in,
    rest, pg, look, terms,
    load_sem, small_sem, s1, f1, r1, q1, s2, r2, s5, r5, s4, r4, s3, f3, r3, q3,
):
    o = lax.axis_index("bkt")
    h = lax.axis_index("grp")
    zh = h // 2
    core = h % 2
    sibling = zh * 2 + (1 - core)

    def far_first(i):
        return (2 + i) * (1 - i // 2) + (3 - i) * (i // 2)

    def owner_at(d):
        y = (o // 8 + far_first(d // 8)) % 4
        z = (o // 4 + 1 - d % 2) % 2
        x = (o + far_first((d // 2) % 4)) % 4
        return y * 8 + z * 4 + x

    def load(c):
        part = pl.ds(c * CHUNK, CHUNK)
        return pltpu.make_async_copy(tiles_hbm.at[part], tiles.at[part], load_sem.at[c])

    for c in range(N_CHUNK):
        load(c).start()

    small = [
        pltpu.make_async_copy(src, dst, small_sem.at[i])
        for i, (src, dst) in enumerate(
            ((row_hbm, row_ref), (col_hbm, col_ref), (move_hbm, move_ref), (pair_hbm, pair_ref))
        )
    ]
    for copy in small:
        copy.start()

    barrier = pltpu.get_barrier_semaphore()

    for j in (2, 1, 3):
        peer = ((zh + j) % N_ZH) * 2 + core
        pl.semaphore_signal(barrier, inc=1, device_id=(o, peer), device_id_type=pl.DeviceIdType.MESH)

    for d in range(N_BKT - 1):
        pl.semaphore_signal(barrier, inc=1, device_id=(owner_at(d), h), device_id_type=pl.DeviceIdType.MESH)

    pl.semaphore_signal(barrier, inc=1, device_id=(o, sibling), device_id_type=pl.DeviceIdType.MESH)

    for copy in small:
        copy.wait()

    row = row_ref[...]
    live = row >= 0
    seg_row = jnp.where(live, (row >> 3) * QT + col_ref[...], -1)
    moving = jnp.zeros_like(row)
    for r in range(BPO * RTG):
        moving = jnp.where(row == r, move_ref[r // RTG, r % RTG], moving)
    wide[...] = jnp.full(wide.shape, -1, i32)
    wide[:, :KT] = jnp.where(live, seg_row + MOVED * moving, -1)
    place = iota((META, TILE), 0)
    meta = jnp.where(place == 0, wide[:, :TILE], jnp.where(place == 1, wide[:, TILE:], -1))
    gath[h, 0:META, :] = meta.astype(i16)

    def column_sums(c):
        load(c).wait()

        for k in range(c * CHUNK, (c + 1) * CHUNK, META):
            sums = jnp.sum(tiles[k : k + META].astype(f32), axis=1)
            gath[h, META + k : 2 * META + k, :] = to_code(sums, SUM_SCALE)

    order = (2, 1, 3)

    def arrived(j):
        return ((zh + N_ZH - j) % N_ZH) * 2 + core

    def arrived_other(j):
        return ((zh + N_ZH - j) % N_ZH) * 2 + (1 - core)

    def hop(buf, part, block, to, send_sem, recv_sem):
        ref = buf.at[block, part]
        return pltpu.make_async_remote_copy(
            src_ref=ref, dst_ref=ref, send_sem=send_sem, recv_sem=recv_sem,
            device_id=(o, to), device_id_type=pl.DeviceIdType.MESH,
        )

    def send_own(buf, part, x, send, forward, recv, other):
        for j in order:
            hop(buf, part, h, ((zh + j) % N_ZH) * 2 + core, send.at[x, j], recv.at[x, j]).start()
        hop(buf, part, h, sibling, forward.at[x, 0], other.at[x, 0]).start()

    def pass_on(buf, part, x, j, send, forward, recv, other):
        hop(buf, part, arrived(j), sibling, send.at[x, j], recv.at[x, j]).wait_recv()
        hop(buf, part, arrived(j), sibling, forward.at[x, j], other.at[x, j]).start()

    def from_other(buf, part, x, j, forward, other):
        hop(buf, part, arrived_other(j), sibling, forward.at[x, j], other.at[x, j]).wait_recv()

    def all_sent(buf, part, x, send, forward, recv, other):
        for j in order:
            hop(buf, part, h, ((zh + j) % N_ZH) * 2 + core, send.at[x, j], recv.at[x, j]).wait_send()
        for j in range(N_ZH):
            hop(buf, part, arrived(j), sibling, forward.at[x, j], other.at[x, j]).wait_send()

    def in_order(i):
        return i + (i // 2) * (5 - 2 * i)

    first = (gath, pl.ds(0, BLK), 0, s1, f1, r1, q1)

    for c in range(N_CHUNK):
        column_sums(c)
    pl.semaphore_wait(barrier, (N_BKT - 1) + (N_ZH - 1) + 1)
    send_own(*first)

    diagonal = iota((KT, KT), 0) == iota((KT, KT), 1)
    seg_col = jnp.sum(jnp.where(diagonal, seg_row.astype(f32), 0.0), axis=1, keepdims=True).astype(i32)
    acc[...] = jnp.zeros_like(acc)
    place = iota((SEG, KT), 0)
    far = arrived(2)
    wanted = (place // QM) * QT + h * QM + place % QM
    wanted_far = wanted + (far - h) * QM

    partner_owner = [pair_ref[o * BPO + p] // BPO for p in range(BPO)]

    slot_ref[o] = 0

    @pl.loop(0, N_BKT - 1)
    def _(d):
        to = owner_at(d)
        pick = 0
        for p in range(BPO):
            pick = jnp.where(partner_owner[p] == to, p, pick)
        pick_ref[d] = pick
        y = (o // 8 + 4 - far_first(d // 8)) % 4
        z = (o // 4 + 1 - d % 2) % 2
        x = (o + 4 - far_first((d // 2) % 4)) % 4
        slot_ref[y * 8 + z * 4 + x] = d

    def count(m):
        code = gath[m, META:BLK, :].astype(i32) + HALF
        high = (code >> 8).astype(f32).astype(bf16)
        low = (code & 255).astype(f32).astype(bf16)
        parts = jnp.concatenate([high, low], axis=1)
        meta = gath[m, 0:META, :].astype(i32)
        theirs = jnp.concatenate([meta[0:1], meta[1:2]], axis=1)[:, :KT]
        moved = theirs >= MOVED
        seg = jnp.where(moved, theirs - MOVED, theirs)
        hit = jnp.where(wanted == seg, 1.0, 0.0)
        hit_moved = jnp.where(moved, hit, 0.0)
        hit_far = jnp.where(wanted_far == seg, 1.0, 0.0)
        mine = jnp.where(seg_col == seg, 1.0, 0.0)
        table = jnp.concatenate([hit, hit_far, hit_moved, mine], axis=0).astype(bf16)
        acc[...] += jnp.dot(table, parts, preferred_element_type=f32)

    @pl.loop(0, KT // 4)
    def _(g):
        for b in range(2):
            for a in range(2):
                turned[g, a * TILE : (a + 1) * TILE, b * TILE : (b + 1) * TILE] = tiles[4 * g + 2 * b + a].T

    @pl.loop(0, N_ZH)
    def _(i):
        count(arrived(in_order(i)))

        @pl.when(i < N_ZH - 1)
        def _():
            j = in_order(i + 1)
            pass_on(*first[:3], j, *first[3:])

        j = in_order(i)
        from_other(*first[:3], j, f1, q1)
        count(arrived_other(j))

    total = acc[:, :TILE] * (256.0 / SUM_SCALE) + acc[:, TILE:] * (1.0 / SUM_SCALE)
    counts = total[:SEG]
    deltas = total[2 * SEG : 3 * SEG]
    panels[:, 0:QM, :] = jnp.exp(-survival_rate * counts).astype(bf16).reshape(BPO, QM, TILE)

    def swap(outbox, inbox, d, send, recv):
        return pltpu.make_async_remote_copy(
            src_ref=outbox.at[d], dst_ref=inbox.at[d], send_sem=send.at[0], recv_sem=recv.at[0],
            device_id=(owner_at(d), h), device_id_type=pl.DeviceIdType.MESH,
        )

    def all_swaps(outbox, inbox, send, recv):
        return pltpu.make_async_remote_copy(
            src_ref=outbox, dst_ref=inbox, send_sem=send.at[0], recv_sem=recv.at[0],
            device_id=(owner_at(0), h), device_id_type=pl.DeviceIdType.MESH,
        )

    for d in range(N_BKT - 1):
        panel_out[d] = panels[pick_ref[d], 0:QM]
        swap(panel_out, panel_in, d, s2, r2).start()

    far_panels = jnp.exp(-survival_rate * total[SEG : 2 * SEG]).astype(bf16)
    panels[:, QM : 2 * QM, :] = far_panels.reshape(BPO, QM, TILE)

    for d in range(N_BKT - 1):
        far_out[d] = panels[pick_ref[d], QM : 2 * QM]
        swap(far_out, far_in, d, s5, r5).start()

    factors[...] = to_code(jnp.exp(-survival_rate * deltas), UNIT_SCALE).reshape(BPO, QM, TILE)

    rest[...] = jnp.exp(-survival_rate * (counts - deltas))
    own[...] = jnp.exp(-survival_rate * total[3 * SEG :]).astype(bf16).astype(f32)
    look[...] = jnp.zeros_like(look)

    source = [slot_ref[partner_owner[p]] for p in range(BPO)]
    all_swaps(panel_out, panel_in, s2, r2).wait_recv()

    for p in range(BPO):
        part = slice(p * QM, (p + 1) * QM)
        pg[h, part, :] = panel_in[source[p]]

    near = (1, 3)
    for j in near:
        hop(pg, pl.ds(0, SEG), h, ((zh + j) % N_ZH) * 2 + core, s3.at[j], r3.at[j]).start()

    def to_other(j):
        return hop(pg, pl.ds(0, SEG), arrived(j), sibling, f3.at[j], q3.at[j])

    def at_other(j):
        return hop(pg, pl.ds(0, SEG), arrived_other(j), sibling, f3.at[j], q3.at[j])

    to_other(0).start()

    all_swaps(far_out, far_in, s5, r5).wait_recv()

    for p in range(BPO):
        pg[far, p * QM : (p + 1) * QM, :] = far_in[source[p]]

    to_other(2).start()

    for d in range(N_BKT - 1):
        factor_out[d] = factors[pick_ref[d]]
        swap(factor_out, factor_in, d, s4, r4).start()

    place3 = iota((KT, SEG), 1)
    base = (place3 // QM) * QT + place3 % QM

    def fetch(m):
        table = jnp.where(base == seg_col - m * QM, 1.0, 0.0).astype(bf16)
        look[...] += jnp.dot(table, pg[m], preferred_element_type=f32)

    @pl.loop(0, 2)
    def _(i):
        fetch(arrived(2 * i))
        at_other(2 * i).wait_recv()
        fetch(arrived_other(2 * i))

    all_sent(*first)
    all_swaps(panel_out, panel_in, s2, r2).wait_send()
    all_swaps(far_out, far_in, s5, r5).wait_send()
    for j in near:
        hop(pg, pl.ds(0, SEG), arrived(j), sibling, s3.at[j], r3.at[j]).wait_recv()
        to_other(j).start()

    @pl.loop(0, 2)
    def _(i):
        fetch(arrived(2 * i + 1))

    @pl.loop(0, 2)
    def _(i):
        at_other(2 * i + 1).wait_recv()
        fetch(arrived_other(2 * i + 1))

    lane = iota((2 * RTG, TILE), 0) % RTG
    even = lane % 2 == 0
    across = (lane // 2) % 2
    down = lane // 4

    @pl.loop(0, KT // (4 * RTG))
    def _(g):
        for x in range(4):
            k = pl.multiple_of(g * 4 * RTG + x * RTG, RTG)
            pair = jnp.concatenate([own[pl.ds(k, RTG), :], look[pl.ds(k, RTG), :]], axis=0)
            split = jnp.concatenate([jnp.where(even, pair, 0.0), jnp.where(even, 0.0, pair)], axis=1).astype(bf16)
            both = jnp.zeros((2 * RTG, TILE), f32)
            for y in range(2):
                got = jnp.dot(split, turned[g * RTG + x * 2 + y], preferred_element_type=f32)
                got = jnp.where(across == 0, got[:, :TILE], got[:, TILE:])
                both = jnp.where(down == y, got, both)
            terms[pl.ds(k, RTG), :] = both[:RTG] - both[RTG:]

    spread = jnp.where(iota((BPO * RTG, KT), 0) == row, 1.0, 0.0).astype(bf16)
    term = terms[...]
    high = term.astype(bf16)
    term = term - high.astype(f32)
    mid = term.astype(bf16)
    low = (term - mid.astype(f32)).astype(bf16)
    summed = jnp.dot(spread, jnp.concatenate([high, mid, low], axis=1), preferred_element_type=f32)
    gains_ref[...] = survival_rate * (summed[:, :TILE] + summed[:, TILE : 2 * TILE] + summed[:, 2 * TILE :])

    all_swaps(factor_out, factor_in, s4, r4).wait_recv()

    for p in range(BPO):
        part = slice(p * QM, (p + 1) * QM)
        got = (factor_in[source[p]].astype(i32) + HALF).astype(f32) * (1.0 / UNIT_SCALE)
        rest[part, :] = rest[part, :] * got

    for t in range(QM):
        panel_ref[:, t * TILE : (t + 1) * TILE] = rest[pl.ds(t, BPO, stride=QM), :]

    for j in near:
        hop(pg, pl.ds(0, SEG), h, ((zh + j) % N_ZH) * 2 + core, s3.at[j], r3.at[j]).wait_send()
    for j in range(N_ZH):
        to_other(j).wait_send()

    all_swaps(factor_out, factor_in, s4, r4).wait_send()


def hand_over(panel_ref, gains_ref, panel_out, gains_out):
    panel_out[...] = panel_ref[...]
    gains_out[...] = gains_ref[...]


def local(record_tiles, tile_row, tile_col, move_blocks, pairing):
    vmem = pl.BlockSpec(memory_space=pltpu.VMEM)
    hbm = pl.BlockSpec(memory_space=pltpu.HBM)
    dma = pltpu.SemaphoreType.DMA
    panel, gains = pl.pallas_call(
        kernel,
        out_shape=(
            jax.ShapeDtypeStruct((BPO, QM * TILE), f32),
            jax.ShapeDtypeStruct((BPO * RTG, TILE), f32),
        ),
        in_specs=[hbm] * 5,
        out_specs=(vmem, vmem),
        scratch_shapes=[
            pltpu.VMEM((1, KT), i32),
            pltpu.VMEM((1, KT), i32),
            pltpu.SMEM((BPO, RTG), i32),
            pltpu.SMEM((N_BKT * BPO,), i32),
            pltpu.SMEM((N_BKT,), i32),
            pltpu.SMEM((N_BKT,), i32),
            pltpu.VMEM((KT, TILE, TILE), bf16),
            pltpu.VMEM((KT // 4, 2 * TILE, 2 * TILE), bf16),
            pltpu.VMEM((1, 2 * TILE), i32),
            pltpu.VMEM((N_GRP, BLK, TILE), i16),
            pltpu.VMEM((3 * SEG + KT, 2 * TILE), f32),
            pltpu.VMEM((KT, TILE), f32),
            pltpu.VMEM((BPO, 2 * QM, TILE), bf16),
            pltpu.VMEM((BPO, QM, TILE), i16),
            pltpu.VMEM((N_BKT - 1, QM, TILE), bf16),
            pltpu.VMEM((N_BKT - 1, QM, TILE), bf16),
            pltpu.VMEM((N_BKT - 1, QM, TILE), i16),
            pltpu.VMEM((N_BKT - 1, QM, TILE), bf16),
            pltpu.VMEM((N_BKT - 1, QM, TILE), bf16),
            pltpu.VMEM((N_BKT - 1, QM, TILE), i16),
            pltpu.VMEM((SEG, TILE), f32),
            pltpu.VMEM((N_GRP, SEG, TILE), bf16),
            pltpu.VMEM((KT, TILE), f32),
            pltpu.VMEM((KT, TILE), f32),
            dma((N_CHUNK,)),
            dma((4,)),
            dma((1, N_ZH)), dma((1, N_ZH)), dma((1, N_ZH)), dma((1, N_ZH)),
            dma((1,)), dma((1,)), dma((1,)), dma((1,)), dma((1,)), dma((1,)),
            dma((N_ZH,)), dma((N_ZH,)), dma((N_ZH,)), dma((N_ZH,)),
        ],
        compiler_params=pltpu.CompilerParams(
            collective_id=0, has_side_effects=True, vmem_limit_bytes=VMEM_BYTES
        ),
        name="swap_round",
    )(record_tiles, tile_row.reshape(1, KT), tile_col.reshape(1, KT), move_blocks, pairing)
    return pl.pallas_call(
        hand_over,
        out_shape=(
            jax.ShapeDtypeStruct((BPO, QM * TILE), f32),
            jax.ShapeDtypeStruct((BPO, RTG, TILE), f32),
        ),
        in_specs=[vmem, vmem],
        out_specs=(vmem, vmem),
        compiler_params=pltpu.CompilerParams(vmem_limit_bytes=VMEM_BYTES),
        name="hand_over",
    )(panel, gains.reshape(BPO, RTG, TILE))


def solution(mesh):
    placed = (
        P(("bkt", "grp"), None, None),
        P(("bkt", "grp")),
        P(("bkt", "grp")),
        P("bkt", "grp"),
        P(),
    )
    return jax.shard_map(
        local,
        mesh=mesh,
        in_specs=placed,
        out_specs=(P("bkt", "grp"), P("bkt", "grp", None)),
        check_vma=False,
    )
```
